512 devices in a mesh: items: 64 (over x, z_hi, y), codes: 8 (over z_lo, core).
Axes of the slice: x: 4, y: 4, z: 16 (z_hi: 4, z_lo: 4; z = z_hi * 4 + z_lo), core: 2. Of those that a mesh axis runs over, the one named last changes fastest.
Arguments:
- block_two: bfloat16 [65536, 1024], P('items'), may hold values from -16 to 16
- block_one: bfloat16 [65536, 1024], P('items'), may hold values from -16 to 16
- codebook_two: bfloat16 [8192, 1024], P('codes', 'items'), may hold values from -6 to 6
- codebook_one: bfloat16 [8192, 1024], P('codes', 'items'), may hold values from -6 to 6
Outputs:
- rebuilt: bfloat16 [65536, 1024], P('items', 'codes')
- next_log_scale: float32 [8192], P('codes')
The draws below stay inside these ranges and needn't reach their ends.
All inputs are finite; a program needn't handle non-finite values.
Results may differ from the reference program's by a relative error of at most 0.015.
Values may be sent and summed in bfloat16 or wider, within the bound.
No kernel may reach another device: no remote copies, remote signals or barrier semaphores. Data moves between devices by JAX's collectives and lax.ppermute only.
A program may use at most 64 MiB of HBM per device.

```python
import math
import jax
import jax.numpy as jnp
from jax import lax

D = 1024
K = 8192
ROWS = 1024
SWEEPS = 3
ITEMS = 65536
N_ITEMS = 64
N_CODES = 8


def shape_items(base_values, key, common_weight, scale_low, scale_high):
    common_key, scale_key = jax.random.split(key)
    groups = ITEMS // ROWS
    common = jax.random.truncated_normal(common_key, -4.0, 4.0, (groups, D), jnp.float32)
    row_index = jnp.arange(ITEMS, dtype=jnp.int32)
    shared = common[row_index // ROWS]
    position = row_index.astype(jnp.float32) / float(ITEMS)
    log_scale = jax.random.uniform(scale_key, (ITEMS,), jnp.float32, math.log(scale_low), math.log(scale_high))
    scales = jnp.exp(log_scale) * (1.0 + position)
    return (scales[:, None] * (base_values + common_weight * shared)).astype(jnp.bfloat16)


def draw_block_two(key, part):
    key = jax.random.fold_in(key, 11)
    base_key, rest_key = jax.random.split(key)
    base_values = jax.random.truncated_normal(base_key, -4.0, 4.0, (ITEMS, D), jnp.float32)
    return shape_items(base_values, rest_key, 0.6, 0.5, 1.0)


def draw_block_one(key, part):
    key = jax.random.fold_in(key, 23)
    base_key, rest_key = jax.random.split(key)
    base_values = jax.random.truncated_normal(base_key, -4.0, 4.0, (ITEMS, D), jnp.float32)
    return shape_items(base_values, rest_key, 0.6, 0.5, 1.0)


def level_of(own_key, shape, cuts, smallest, high):
    def one(axis_at, parts):
        steps = jax.random.uniform(jax.random.fold_in(jax.random.fold_in(own_key, 6), axis_at), (parts,), jnp.float32, smallest / len(cuts), high / len(cuts))
        return jnp.repeat(jnp.exp(steps), shape[axis_at] // parts).reshape((-1,) + (1,) * (len(shape) - axis_at - 1))

    level = one(*cuts[0])
    for cut in cuts[1:]:
        level = level * one(*cut)
    return level


def noise(key, shape, width, most, pieces=(), held_as=jnp.bfloat16):
    drawn = jax.random.normal(key, shape, jnp.float32) * width
    if len(pieces) > 0:
        drawn = level_of(key, shape, pieces, -0.22, 0.18) * drawn
    return jnp.clip(drawn, min=-most, max=most).astype(held_as)


def setup_inputs(seed: int = 0) -> dict:
    streams_of = jax.random.split(jax.random.key(seed), 5)
    return {
        "block_two": draw_block_two(jax.random.fold_in(streams_of[4], 71), 0),
        "block_one": draw_block_one(jax.random.fold_in(streams_of[4], 71), 0),
        "codebook_two": noise(streams_of[2], (K, D), 1.0, 6.0, ((0, 8), (1, 64))),
        "codebook_one": noise(streams_of[3], (K, D), 1.0, 6.0, ((0, 8), (1, 64))),
    }


def contract(left_rows, right_rows):
    return lax.dot_general(left_rows, right_rows, (((1,), (1,)), ((), ())), preferred_element_type=jnp.float32)

def kernel_rows(row_block, codebook, squares):
    scores = contract(row_block, codebook)
    return jnp.exp((scores - 0.5 * squares[None, :]) * (1.0 / math.sqrt(D)))

def reference(block_two, block_one, codebook_two, codebook_one):
    target = float(ITEMS) / float(K)
    norms_two = lax.optimization_barrier(jnp.sum(jnp.square(codebook_two.astype(jnp.float32)), axis=1))
    norms_one = lax.optimization_barrier(jnp.sum(jnp.square(codebook_one.astype(jnp.float32)), axis=1))
    grouped_two = block_two.reshape(N_ITEMS, ROWS, D)
    kernel_two = lax.map(lambda row_block: kernel_rows(row_block, codebook_two, norms_two), grouped_two).reshape(ITEMS, K)
    col_scale = jnp.ones((K,), jnp.float32)
    for sweep_index in range(SWEEPS):
        row_scale = 1.0 / jnp.dot(kernel_two, col_scale, precision=lax.Precision.HIGHEST)
        col_scale = target / jnp.dot(row_scale, kernel_two, precision=lax.Precision.HIGHEST)
    row_scale = 1.0 / jnp.dot(kernel_two, col_scale, precision=lax.Precision.HIGHEST)
    transport = (row_scale[:, None] * kernel_two * col_scale[None, :]).astype(jnp.bfloat16)
    code_width = K // N_CODES
    running = jnp.zeros((ITEMS, D), jnp.float32)
    for shard_index in range(N_CODES):
        first_code = shard_index * code_width
        partial_value = jnp.dot(transport[:, first_code:first_code + code_width], codebook_two[first_code:first_code + code_width], preferred_element_type=jnp.float32)
        running = running + lax.optimization_barrier(partial_value.astype(jnp.bfloat16)).astype(jnp.float32)
    rebuilt = running.astype(jnp.bfloat16)
    grouped_one = block_one.reshape(N_ITEMS, ROWS, D)
    row_totals = lax.map(lambda row_block: lax.optimization_barrier(jnp.sum(kernel_rows(row_block, codebook_one, norms_one), axis=1)), grouped_one)
    weights_one = 1.0 / row_totals

    def add_columns(running_cols, inputs):
        row_block, weights = inputs
        kernel_part = kernel_rows(row_block, codebook_one, norms_one)
        return (running_cols + jnp.dot(weights, kernel_part, precision=lax.Precision.HIGHEST), None)
    column_total, unused = lax.scan(add_columns, jnp.zeros((K,), jnp.float32), (grouped_one, weights_one))
    next_log_scale = math.log(target) - jnp.log(column_total)
    return (rebuilt, next_log_scale)
```

```python
import functools
import math

import jax
import jax.numpy as jnp
from jax import lax
from jax.experimental import pallas as pl
from jax.experimental.pallas import tpu as pltpu
from jax.sharding import PartitionSpec as P

SWEEPS = 3
RING = 4
PLANE = ("x", "y")
CODES = ("z_lo", "core")
ITEMS = ("x", "z_hi", "y")
MIB = 1 << 20
STEP = 256
MOST = 48 * MIB
HBM = pl.BlockSpec(memory_space=pltpu.HBM)
FULL = pl.BlockSpec(memory_space=pltpu.VMEM)
BF16 = jnp.bfloat16
F32 = jnp.float32


def call(body, outs, name, ins, flops=0, nbytes=4 * MIB, limit=16 * MIB, scratch=(), out_specs=None):
    ins = [i if isinstance(i, tuple) else (i, FULL) for i in ins]
    specs = {} if out_specs is None else {"out_specs": out_specs}
    return pl.pallas_call(
        body,
        out_shape=outs,
        in_specs=[spec for _, spec in ins],
        scratch_shapes=list(scratch),
        compiler_params=pltpu.CompilerParams(vmem_limit_bytes=limit),
        cost_estimate=pl.CostEstimate(flops=flops, bytes_accessed=nbytes, transcendentals=0),
        name=name,
        **specs,
    )(*[array for array, _ in ins])


def shape(*sizes, of=F32):
    return jax.ShapeDtypeStruct(sizes, of)


def spread(rows, count):
    return jnp.broadcast_to(rows[None], (count,) + rows.shape)


def nt(a, b):
    return lax.dot_general(a, b, (((1,), (1,)), ((), ())), preferred_element_type=F32)


def nn(a, b):
    return jnp.dot(a, b, preferred_element_type=F32)


def k_rows(block, book, norms, inv_root):
    scores = nn(block, book)
    return jnp.exp((scores - norms) * inv_root).astype(BF16)


def fan_body(copies, column, two, one):
    run = column.shape[1] // 2
    for z in range(column.shape[0]):
        one[z] = column[z, run:, :]
        for i in range(copies):
            two[i, z] = column[z, :run, :]


def fetch_book(came, book, sems):
    fetches = []
    for x in range(RING):
        for y in range(RING):
            move = pltpu.make_async_copy(came.at[x * RING + y], book.at[x, :, y], sems.at[x * RING + y])
            move.start()
            fetches.append(move)
    return fetches


def half_norms(book, fetches):
    acc = jnp.zeros(book.shape[3:], F32)
    for x in range(RING):
        for y in range(RING):
            fetches[x * RING + y].wait()
            for z in range(RING):
                wide = book[x, z, y].astype(F32)
                acc = acc + wide * wide
    return 0.5 * jnp.sum(acc, axis=0, keepdims=True)


def make_k(inv_root, groups, came, block, k, total, book, held, sems, after_step=None):
    rows, features = block.shape
    codes = book.shape[-1]
    fetches = fetch_book(came, book, sems)
    loads = []
    for i in range(rows // STEP):
        here = pl.ds(i * STEP, STEP)
        loads.append(pltpu.make_async_copy(block.at[here], held.at[here], sems.at[len(fetches) + i]))
        loads[-1].start()
    norms = half_norms(book, fetches)
    ones = jnp.ones((16, codes), BF16)
    for i, load in enumerate(loads):
        here = slice(i * STEP, (i + 1) * STEP)
        load.wait()
        values = k_rows(held[here, :], book[...].reshape(features, codes), norms, inv_root)
        k[here, :] = values
        total[:, :, here] = spread(nt(ones, values)[0:1], groups)
        if after_step is not None:
            after_step(i)


def kernel_two_body(inv_root, groups, came, block, k_out, total, book, held, sems):
    make_k(inv_root, groups, came, block, k_out, total, book, held, sems)


def kernel_one_body(inv_root, groups, came, block, after, k_out, total, book, held, k, sems, saved):
    saves = []

    def save(i):
        here = pl.ds(i * STEP, STEP)
        saves.append(pltpu.make_async_copy(k.at[here], k_out.at[here], saved.at[i]))
        saves[-1].start()

    make_k(inv_root, groups, came, block, k, total, book, held, sems, save)
    for move in saves:
        move.wait()


def two_terms(row):
    high = row.astype(BF16).astype(F32)
    at = lax.broadcasted_iota(jnp.int32, (16, row.shape[1]), 0)
    return jnp.where(at == 0, high, jnp.where(at == 1, row - high, 0.0)).astype(BF16)


def over_codes(scale, k):
    return jnp.sum(nt(two_terms(scale), k[...]), axis=0, keepdims=True)


def over_items(scale, k):
    return jnp.sum(nn(two_terms(scale), k[...]), axis=0, keepdims=True)


def col_body(copies, gathered, k, col_out, scale_out):
    scale = 1.0 / jnp.sum(gathered[...], axis=0)
    scale_out[...] = scale
    col_out[...] = spread(over_items(scale, k), copies)


def both_cols_body(copies, gathered, k, k_one, col_out, scale_out, held, sem):
    fetch = pltpu.make_async_copy(k_one, held, sem)
    fetch.start()
    scale = 1.0 / jnp.sum(gathered[...], axis=0)
    scale_out[...] = scale[0:1]
    col_out[:, 0:1, :] = spread(over_items(scale[0:1], k), copies)
    fetch.wait()
    col_out[:, 1:2, :] = spread(over_items(scale[1:2], held), copies)


def row_body(target, groups, cols, k, *refs):
    out = refs[-1]
    scale = target / jnp.sum(cols[...], axis=0)[0:1]
    out[:, 0:1, :] = spread(over_codes(scale, k), groups)
    for more in refs[:-1]:
        out[:, 1:2, :] = more[...]


def halves(row):
    high = row.astype(BF16)
    return high, (row - high.astype(F32)).astype(BF16)


def cut(row, width):
    return jnp.concatenate([row[:, i : i + width] for i in range(0, row.shape[1], width)], 0)


def fetch_parity(came, picked, parity, sems):
    fetches = []
    for x in range(RING):
        for y in range(RING):
            here = came.at[x * RING + y, pl.ds(2 * parity, 2)]
            move = pltpu.make_async_copy(here, picked.at[x, :, y], sems.at[x * RING + y])
            move.start()
            fetches.append(move)
    return fetches


def transport_body(target, cols, r, k, came, t_out, other_out, sums_out, picked, sems):
    rows, codes = k.shape
    wide = other_out.shape[1]
    fetches = fetch_parity(came, picked, 1 - lax.axis_index("core"), sems)
    scale = target / jnp.sum(cols[...], axis=0)[0:1]
    sums = over_codes(scale, k)
    sums_out[...] = sums
    parts = jnp.concatenate([cut(part.astype(F32), wide) for part in halves(sums)], 0)
    filled = jnp.concatenate([parts, jnp.zeros((16 - parts.shape[0], wide), F32)], 0)
    other_out[rows : rows + 16, :] = filled.astype(BF16)
    r_up = jnp.transpose(jnp.broadcast_to(r[0:1, :], (8, r.shape[1])))
    for fetch in fetches:
        fetch.wait()
    for i in range(rows // STEP):
        here = slice(i * STEP, (i + 1) * STEP)
        t = (r_up[here, 0:1] * k[here, :].astype(F32) * scale).astype(BF16)
        t_out[here, :] = t
        other_out[here, :] = nt(t, picked[...].reshape(wide, codes)).astype(BF16)


def mine_body(t, came, out, picked, sems):
    wide = out.shape[1]
    for fetch in fetch_parity(came, picked, lax.axis_index("core"), sems):
        fetch.wait()
    for i in range(t.shape[0] // STEP):
        here = slice(i * STEP, (i + 1) * STEP)
        out[here, :] = nt(t[here, :], picked[...].reshape(wide, t.shape[1]))


def pack(sums):
    return jnp.concatenate([part.astype(F32) for part in halves(sums)], 0).astype(BF16)


def unpack(tail):
    tail = tail.astype(F32)
    return tail[:8] + tail[8:]


def pair_body(mine, came, sums, here_out, far_out, sums_out, cross_out, beside_out):
    rows, wide = mine.shape
    width = wide // RING
    tail = came[rows : rows + 16, :].astype(F32)
    n = rows // wide
    theirs = [tail[i : i + 1, :] + tail[n + i : n + i + 1, :] for i in range(n)]
    both = cut(sums[...] + jnp.concatenate(theirs, 1), width)
    sums_out[...] = both
    z = lax.axis_index("z_lo")
    pair = z + 1 - 2 * (z % 2)
    far = (z + 2) % RING
    for chip, out in ((z, here_out), (far, far_out), ((pair + 2) % RING, cross_out), (pair, beside_out)):
        lanes = pl.ds(pl.multiple_of(chip * width, width), width)
        value = mine[:, lanes] + came[:rows, lanes].astype(F32)
        out[:rows, :] = value.astype(out.dtype)
    cross_out[rows : rows + 16, :] = pack(both)


def cross_body(far, came, sums, out, sums_out):
    rows = far.shape[0]
    out[:rows, :] = (far[...] + came[:rows, :].astype(F32)).astype(BF16)
    both = sums[...] + unpack(came[rows : rows + 16, :])
    sums_out[...] = both
    out[rows : rows + 16, :] = pack(both)


def last_body(own, beside, far, sums, r, out):
    rows, width = out.shape
    total = sums[...] + unpack(far[rows : rows + 16, :])
    ratio = jnp.transpose(1.0 / (cut(r[0:1, :], width) * total))
    for i in range(rows // width):
        here = slice(i * width, (i + 1) * width)
        value = own[here, :] + beside[here, :].astype(F32) + far[here, :].astype(F32)
        out[here, :] = (value * ratio[:, i : i + 1]).astype(out.dtype)


def shards(block_two, block_one, codebook_two, codebook_one):
    rows, features = block_two.shape
    codes, run = codebook_two.shape
    groups = lax.axis_size(CODES)
    target = float(rows * lax.axis_size(ITEMS)) / float(codes * groups)
    inv_root = 1.0 / math.sqrt(features)
    book_flops = 2 * rows * features * codes

    plane = RING * RING
    sem = pltpu.SemaphoreType.DMA
    steps = rows // STEP
    both_books = spread(jnp.concatenate([codebook_two.T, codebook_one.T], 0), RING)
    column = lax.all_to_all(both_books, "z_hi", 0, 0)
    two, one = call(
        functools.partial(fan_body, plane),
        (shape(plane, RING, run, codes, of=BF16), shape(RING, run, codes, of=BF16)),
        "fan",
        [column],
    )
    came_two = lax.all_to_all(two, PLANE, 0, 0)
    came_two, one = lax.optimization_barrier((came_two, one))
    came_one = lax.all_gather(one, PLANE, axis=0, tiled=False)
    book_room = [
        pltpu.VMEM((RING, RING, RING, run, codes), BF16),
        pltpu.VMEM((rows, features), BF16),
    ]
    k_two, row_sums = call(
        functools.partial(kernel_two_body, inv_root, groups),
        (shape(rows, codes, of=BF16), shape(groups, 1, rows)),
        "kernel_two",
        [(came_two, HBM), (block_two, HBM)],
        flops=book_flops,
        limit=MOST,
        scratch=book_room + [sem((plane + steps,))],
    )

    def make_k_one(after):
        return call(
            functools.partial(kernel_one_body, inv_root, groups),
            (shape(rows, codes, of=BF16), shape(groups, 1, rows)),
            "kernel_one",
            [(came_one, HBM), (block_one, HBM), (after, HBM)],
            flops=book_flops,
            limit=MOST + 2 * MIB,
            scratch=book_room + [pltpu.VMEM((rows, codes), BF16), sem((plane + steps,)), sem((steps,))],
            out_specs=(HBM, FULL),
        )

    more = []
    small = 32 * rows * codes
    for sweep in range(SWEEPS):
        last = sweep == SWEEPS - 1
        n = 2 if last else 1
        gathered = lax.all_to_all(row_sums, CODES, 0, 0)
        outs = (shape(plane, n, codes), shape(1, rows))
        if last:
            col, scale = call(
                functools.partial(both_cols_body, plane),
                outs,
                "columns",
                [gathered, k_two, (k_one, HBM)],
                flops=small,
                limit=MOST,
                scratch=[pltpu.VMEM((rows, codes), BF16), sem],
            )
        else:
            col, scale = call(
                functools.partial(col_body, plane), outs, "columns", [gathered, k_two], flops=small
            )
        col = spread(jnp.sum(lax.all_to_all(col, PLANE, 0, 0), axis=0), RING)
        cols = lax.all_to_all(col, "z_hi", 0, 0)
        if sweep == 1:
            k_one, first_one = make_k_one(col)
            more = [first_one]
        if not last:
            row_sums = call(
                functools.partial(row_body, target, groups),
                shape(groups, 1 + len(more), rows),
                "rows",
                [cols, k_two] + more,
                flops=small,
            )

    wide = features // 2
    width = features // groups
    picked = pltpu.VMEM((RING, 2, RING, run, codes), BF16)
    t, other, sums = call(
        functools.partial(transport_body, target),
        (shape(rows, codes, of=BF16), shape(rows + 16, wide, of=BF16), shape(1, rows)),
        "transport",
        [cols, scale, k_two, (came_two, HBM)],
        flops=book_flops // 2,
        limit=MOST - 4 * MIB,
        scratch=[picked, sem((plane,))],
    )
    came = lax.ppermute(other, "core", [(0, 1), (1, 0)])
    mine = call(
        mine_body,
        shape(rows, wide),
        "mine",
        [t, (came_two, HBM)],
        flops=book_flops // 2,
        limit=MOST - 4 * MIB,
        scratch=[picked, sem((plane,))],
    )
    tall = shape(rows + 16, width, of=BF16)
    own, far, sums, cross, beside = call(
        pair_body,
        (shape(rows, width), shape(rows, width), shape(8, width), tall, shape(rows, width, of=BF16)),
        "pair",
        [mine, came, sums],
        limit=24 * MIB,
    )
    neighbours = [(0, 1), (1, 0), (2, 3), (3, 2)]
    crossed = lax.ppermute(cross, "z_lo", neighbours)
    passed, sums = call(cross_body, (tall, shape(8, width)), "cross", [far, crossed, sums])
    passed, beside = lax.optimization_barrier((passed, beside))
    passed = lax.ppermute(passed, "z_lo", [(0, 2), (2, 0), (1, 3), (3, 1)])
    beside = lax.ppermute(beside, "z_lo", neighbours)
    rebuilt = call(
        last_body, shape(rows, width, of=BF16), "last", [own, beside, passed, sums, scale]
    )
    cols_one = jnp.sum(cols[:, 1], axis=0)
    next_log_scale = math.log(target) - jnp.log(cols_one)
    return rebuilt, next_log_scale


def solution(mesh):
    sizes = (RING, RING, RING, RING, 2)
    rings = jax.sharding.Mesh(mesh.devices.reshape(sizes), ("x", "z_hi", "y", "z_lo", "core"))
    block, book = P(ITEMS, None), P(CODES, ITEMS)
    return jax.shard_map(
        shards,
        mesh=rings,
        in_specs=(block, block, book, book),
        out_specs=(P(ITEMS, CODES), P(CODES)),
        check_vma=False,
    )
```

```python
import functools
import math

import jax
import jax.numpy as jnp
from jax import lax
from jax.experimental import pallas as pl
from jax.experimental.pallas import tpu as pltpu
from jax.sharding import PartitionSpec as P

SWEEPS = 3
RING = 4
PLANE = ("x", "y")
CODES = ("z_lo", "core")
ITEMS = ("x", "z_hi", "y")
MIB = 1 << 20
STEP = 256
FEW = 128
MOST = 48 * MIB
HBM = pl.BlockSpec(memory_space=pltpu.HBM)
FULL = pl.BlockSpec(memory_space=pltpu.VMEM)
BF16 = jnp.bfloat16
F32 = jnp.float32


def call(body, outs, name, ins, flops=0, nbytes=4 * MIB, limit=16 * MIB, scratch=(), out_specs=None):
    ins = [i if isinstance(i, tuple) else (i, FULL) for i in ins]
    specs = {} if out_specs is None else {"out_specs": out_specs}
    return pl.pallas_call(
        body,
        out_shape=outs,
        in_specs=[spec for _, spec in ins],
        scratch_shapes=list(scratch),
        compiler_params=pltpu.CompilerParams(vmem_limit_bytes=limit),
        cost_estimate=pl.CostEstimate(flops=flops, bytes_accessed=nbytes, transcendentals=0),
        name=name,
        **specs,
    )(*[array for array, _ in ins])


def shape(*sizes, of=F32):
    return jax.ShapeDtypeStruct(sizes, of)


def spread(rows, count):
    return jnp.broadcast_to(rows[None], (count,) + rows.shape)


def nt(a, b):
    return lax.dot_general(a, b, (((1,), (1,)), ((), ())), preferred_element_type=F32)


def nn(a, b):
    return jnp.dot(a, b, preferred_element_type=F32)


def k_rows(block, book, norms, inv_root):
    scores = nn(block, book)
    return jnp.exp((scores - norms) * inv_root).astype(BF16)


def fan_body(copies, column, two, one):
    run = column.shape[1] // 2
    for z in range(column.shape[0]):
        one[z] = column[z, run:, :]
        for i in range(copies):
            two[i, z] = column[z, :run, :]


def fetch_book(came, book, sems):
    fetches = []
    for x in range(RING):
        for y in range(RING):
            move = pltpu.make_async_copy(came.at[x * RING + y], book.at[x, :, y], sems.at[x * RING + y])
            move.start()
            fetches.append(move)
    return fetches


def half_norms(book, fetches):
    acc = jnp.zeros(book.shape[3:], F32)
    for x in range(RING):
        for y in range(RING):
            fetches[x * RING + y].wait()
            for z in range(RING):
                wide = book[x, z, y].astype(F32)
                acc = acc + wide * wide
    return 0.5 * jnp.sum(acc, axis=0, keepdims=True)


def make_k(inv_root, groups, came, block, k, total, book, held, sems, after_step=None):
    rows, features = block.shape
    codes = book.shape[-1]
    fetches = fetch_book(came, book, sems)
    loads = []
    for i in range(rows // STEP):
        here = pl.ds(i * STEP, STEP)
        loads.append(pltpu.make_async_copy(block.at[here], held.at[here], sems.at[len(fetches) + i]))
        loads[-1].start()
    norms = half_norms(book, fetches)
    ones = jnp.ones((16, codes), BF16)
    for i, load in enumerate(loads):
        here = slice(i * STEP, (i + 1) * STEP)
        load.wait()
        values = k_rows(held[here, :], book[...].reshape(features, codes), norms, inv_root)
        k[here, :] = values
        total[:, :, here] = spread(nt(ones, values)[0:1], groups)
        if after_step is not None:
            after_step(i)


def kernel_two_body(inv_root, groups, came, block, k_out, total, book, held, sems):
    make_k(inv_root, groups, came, block, k_out, total, book, held, sems)


def kernel_one_body(inv_root, groups, came, block, after, k_out, total, book, held, k, sems, saved):
    saves = []

    def save(i):
        here = pl.ds(i * STEP, STEP)
        saves.append(pltpu.make_async_copy(k.at[here], k_out.at[here], saved.at[i]))
        saves[-1].start()

    make_k(inv_root, groups, came, block, k, total, book, held, sems, save)
    for move in saves:
        move.wait()


def two_terms(row):
    high = row.astype(BF16).astype(F32)
    at = lax.broadcasted_iota(jnp.int32, (16, row.shape[1]), 0)
    return jnp.where(at == 0, high, jnp.where(at == 1, row - high, 0.0)).astype(BF16)


def over_codes(scale, k):
    return jnp.sum(nt(two_terms(scale), k[...]), axis=0, keepdims=True)


def over_items(scale, k):
    return jnp.sum(nn(two_terms(scale), k[...]), axis=0, keepdims=True)


def col_body(copies, gathered, k, col_out, scale_out):
    scale = 1.0 / jnp.sum(gathered[...], axis=0)
    scale_out[...] = scale
    col_out[...] = spread(over_items(scale, k), copies)


def both_cols_body(copies, gathered, k, k_one, col_out, scale_out, held, sem):
    fetch = pltpu.make_async_copy(k_one, held, sem)
    fetch.start()
    scale = 1.0 / jnp.sum(gathered[...], axis=0)
    scale_out[...] = scale[0:1]
    col_out[:, 0:1, :] = spread(over_items(scale[0:1], k), copies)
    fetch.wait()
    col_out[:, 1:2, :] = spread(over_items(scale[1:2], held), copies)


def row_body(target, groups, cols, k, *refs):
    out = refs[-1]
    scale = target / jnp.sum(cols[...], axis=0)[0:1]
    out[:, 0:1, :] = spread(over_codes(scale, k), groups)
    for more in refs[:-1]:
        out[:, 1:2, :] = more[...]


def halves(row):
    high = row.astype(BF16)
    return high, (row - high.astype(F32)).astype(BF16)


def cut(row, width):
    return jnp.concatenate([row[:, i : i + width] for i in range(0, row.shape[1], width)], 0)


def fetch_parity(came, picked, parity, sems):
    fetches = []
    for x in range(RING):
        for y in range(RING):
            here = came.at[x * RING + y, pl.ds(2 * parity, 2)]
            move = pltpu.make_async_copy(here, picked.at[x, :, y], sems.at[x * RING + y])
            move.start()
            fetches.append(move)
    return fetches


def weigh(t_out, other_out, picked, k, r, scale, first):
    count, codes = t_out.shape
    wide = other_out.shape[1]
    r_up = jnp.transpose(jnp.broadcast_to(r[0:1, first : first + count], (8, count)))
    for i in range(count // FEW):
        here = slice(i * FEW, (i + 1) * FEW)
        rows = slice(first + i * FEW, first + (i + 1) * FEW)
        t_out[here, :] = (r_up[here, 0:1] * k[rows, :].astype(F32) * scale).astype(BF16)
    yield
    for i in range(count // FEW):
        here = slice(i * FEW, (i + 1) * FEW)
        other_out[here, :] = nt(t_out[here, :], picked[...].reshape(wide, codes)).astype(BF16)
    yield


def transport_body(target, cols, r, k, came, t_out, other_out, sums_out, theirs, ours, sems, our_sems):
    count = t_out.shape[0]
    wide = other_out.shape[1]
    core = lax.axis_index("core")
    fetches = fetch_parity(came, theirs, 1 - core, sems)
    our_fetches = fetch_parity(came, ours, core, our_sems)
    scale = target / jnp.sum(cols[...], axis=0)[0:1]
    sums = over_codes(scale, k)
    sums_out[...] = sums
    parts = jnp.concatenate([cut(part.astype(F32), wide) for part in halves(sums)], 0)
    filled = jnp.concatenate([parts, jnp.zeros((16 - parts.shape[0], wide), F32)], 0)
    other_out[count : count + 16, :] = filled.astype(BF16)
    work = weigh(t_out, other_out, theirs, k, r, scale, 0)
    next(work)
    for fetch in fetches:
        fetch.wait()
    next(work)
    for fetch in our_fetches:
        fetch.wait()


def second_body(target, cols, r, k, theirs, t_out, other_out):
    scale = target / jnp.sum(cols[...], axis=0)[0:1]
    for _ in weigh(t_out, other_out, theirs, k, r, scale, k.shape[0] - t_out.shape[0]):
        pass


def pack(sums):
    return jnp.concatenate([part.astype(F32) for part in halves(sums)], 0).astype(BF16)


def unpack(tail):
    tail = tail.astype(F32)
    return tail[:8] + tail[8:]


def add_cores(t, ours, came, here_out, far_out, near_out, mine):
    count, codes = t.shape
    wide = mine.shape[1]
    width = wide // RING
    for i in range(count // FEW):
        here = slice(i * FEW, (i + 1) * FEW)
        mine[here, :] = nt(t[here, :], ours[...].reshape(wide, codes))
    z = lax.axis_index("z_lo")
    pair = z + 1 - 2 * (z % 2)
    far = (z + 2) % RING
    below = near_out.shape[0] - count
    for chip, out, at in ((z, here_out, 0), (far, far_out, 0), ((pair + 2) % RING, near_out, 0), (pair, near_out, below)):
        lanes = pl.ds(pl.multiple_of(chip * width, width), width)
        value = mine[:, lanes] + came[:count, lanes].astype(F32)
        out[at : at + count, :] = value.astype(out.dtype)


def pair_body(t, ours, came, sums, here_out, far_out, near_out, sums_out, mine):
    add_cores(t, ours, came, here_out, far_out, near_out, mine)
    count, wide = mine.shape
    width = wide // RING
    tail = came[count : count + 16, :].astype(F32)
    n = sums.shape[1] // wide
    theirs = [tail[i : i + 1, :] + tail[n + i : n + i + 1, :] for i in range(n)]
    both = cut(sums[...] + jnp.concatenate(theirs, 1), width)
    sums_out[...] = both
    near_out[count : count + 16, :] = pack(both)


def second_pair_body(t, ours, came, after, here_out, far_out, near_out, mine):
    add_cores(t, ours, came, here_out, far_out, near_out, mine)


def cross_body(far, came, sums, out, sums_out):
    count = far.shape[0]
    out[:count, :] = (far[...] + came[:count, :].astype(F32)).astype(BF16)
    both = sums[...] + unpack(came[count : count + 16, :])
    sums_out[...] = both
    out[count : count + 16, :] = pack(both)


def second_cross_body(far, came, after, out):
    count = far.shape[0]
    out[...] = (far[...] + came[:count, :].astype(F32)).astype(BF16)


def last_body(own, second_own, near, second_near, far, second_far, sums, r, out):
    rows, width = out.shape
    count = own.shape[0]
    total = sums[...] + unpack(far[count : count + 16, :])
    ratio = jnp.transpose(1.0 / (cut(r[0:1, :], width) * total))
    for i in range(rows // width):
        at = i * width
        mine, beside, passed = own, near, far
        if at >= count:
            at -= count
            mine, beside, passed = second_own, second_near, second_far
        below = at + beside.shape[0] - mine.shape[0]
        value = mine[at : at + width, :] + beside[below : below + width, :].astype(F32)
        value = value + passed[at : at + width, :].astype(F32)
        out[i * width : (i + 1) * width, :] = (value * ratio[:, i : i + 1]).astype(out.dtype)


def shards(block_two, block_one, codebook_two, codebook_one):
    rows, features = block_two.shape
    codes, run = codebook_two.shape
    groups = lax.axis_size(CODES)
    target = float(rows * lax.axis_size(ITEMS)) / float(codes * groups)
    inv_root = 1.0 / math.sqrt(features)
    book_flops = 2 * rows * features * codes

    plane = RING * RING
    sem = pltpu.SemaphoreType.DMA
    steps = rows // STEP
    both_books = spread(jnp.concatenate([codebook_two.T, codebook_one.T], 0), RING)
    column = lax.all_to_all(both_books, "z_hi", 0, 0)
    two, one = call(
        functools.partial(fan_body, plane),
        (shape(plane, RING, run, codes, of=BF16), shape(RING, run, codes, of=BF16)),
        "fan",
        [column],
    )
    came_two = lax.all_to_all(two, PLANE, 0, 0)
    came_two, one = lax.optimization_barrier((came_two, one))
    came_one = lax.all_gather(one, PLANE, axis=0, tiled=False)
    book_room = [
        pltpu.VMEM((RING, RING, RING, run, codes), BF16),
        pltpu.VMEM((rows, features), BF16),
    ]
    k_two, row_sums = call(
        functools.partial(kernel_two_body, inv_root, groups),
        (shape(rows, codes, of=BF16), shape(groups, 1, rows)),
        "kernel_two",
        [(came_two, HBM), (block_two, HBM)],
        flops=book_flops,
        limit=MOST + 4 * MIB - MIB // 4,
        scratch=book_room + [sem((plane + steps,))],
    )

    def make_k_one(after):
        return call(
            functools.partial(kernel_one_body, inv_root, groups),
            (shape(rows, codes, of=BF16), shape(groups, 1, rows)),
            "kernel_one",
            [(came_one, HBM), (block_one, HBM), (after, HBM)],
            flops=book_flops,
            limit=MOST + 2 * MIB,
            scratch=book_room + [pltpu.VMEM((rows, codes), BF16), sem((plane + steps,)), sem((steps,))],
            out_specs=(HBM, FULL),
        )

    more = []
    small = 32 * rows * codes
    for sweep in range(SWEEPS):
        last = sweep == SWEEPS - 1
        n = 2 if last else 1
        gathered = lax.all_to_all(row_sums, CODES, 0, 0)
        outs = (shape(plane, n, codes), shape(1, rows))
        if last:
            col, scale = call(
                functools.partial(both_cols_body, plane),
                outs,
                "columns",
                [gathered, k_two, (k_one, HBM)],
                flops=small,
                limit=MOST,
                scratch=[pltpu.VMEM((rows, codes), BF16), sem],
            )
        else:
            col, scale = call(
                functools.partial(col_body, plane), outs, "columns", [gathered, k_two], flops=small
            )
        col = spread(jnp.sum(lax.all_to_all(col, PLANE, 0, 0), axis=0), RING)
        cols = lax.all_to_all(col, "z_hi", 0, 0)
        if sweep == 1:
            k_one, first_one = make_k_one(col)
            more = [first_one]
        if not last:
            row_sums = call(
                functools.partial(row_body, target, groups),
                shape(groups, 1 + len(more), rows),
                "rows",
                [cols, k_two] + more,
                flops=small,
            )

    wide = features // 2
    width = features // groups
    more_rows = rows // 2
    few_rows = rows - more_rows
    parity = (RING, 2, RING, run, codes)
    t, other, sums, theirs, ours = call(
        functools.partial(transport_body, target),
        (
            shape(more_rows, codes, of=BF16),
            shape(more_rows + 16, wide, of=BF16),
            shape(1, rows),
            shape(*parity, of=BF16),
            shape(*parity, of=BF16),
        ),
        "transport",
        [cols, scale, k_two, (came_two, HBM)],
        flops=2 * more_rows * codes * wide,
        limit=MOST + MIB // 4,
        scratch=[sem((plane,)), sem((plane,))],
    )
    swap = [(0, 1), (1, 0)]
    came = lax.ppermute(other, "core", swap)
    second_t, second_other = call(
        functools.partial(second_body, target),
        (shape(few_rows, codes, of=BF16), shape(few_rows, wide, of=BF16)),
        "second_transport",
        [cols, scale, k_two, theirs],
        flops=2 * few_rows * codes * wide,
    )
    second_came = lax.ppermute(second_other, "core", swap)
    own, far, nearing, sums = call(
        pair_body,
        (
            shape(more_rows, width),
            shape(more_rows, width),
            shape(2 * more_rows + 16, width, of=BF16),
            shape(8, width),
        ),
        "pair",
        [t, ours, came, sums],
        flops=2 * more_rows * codes * wide,
        scratch=[pltpu.VMEM((more_rows, wide), F32)],
    )
    neighbours = [(0, 1), (1, 0), (2, 3), (3, 2)]
    across = [(0, 2), (2, 0), (1, 3), (3, 1)]
    near = lax.ppermute(nearing, "z_lo", neighbours)
    second_own, second_far, second_near = call(
        second_pair_body,
        (shape(few_rows, width), shape(few_rows, width), shape(2 * few_rows, width, of=BF16)),
        "second_pair",
        [second_t, ours, second_came, (nearing, HBM)],
        flops=2 * few_rows * codes * wide,
        scratch=[pltpu.VMEM((few_rows, wide), F32)],
    )
    second_near = lax.ppermute(second_near, "z_lo", neighbours)
    passing, sums = call(
        cross_body,
        (shape(more_rows + 16, width, of=BF16), shape(8, width)),
        "cross",
        [far, near, sums],
    )
    passed = lax.ppermute(passing, "z_lo", across)
    second_passed = call(
        second_cross_body,
        shape(few_rows, width, of=BF16),
        "second_cross",
        [second_far, second_near, (passing, HBM)],
        flops=book_flops,
        nbytes=32 * MIB,
    )
    second_passed = lax.ppermute(second_passed, "z_lo", across)
    rebuilt = call(
        last_body,
        shape(rows, width, of=BF16),
        "last",
        [own, second_own, near, second_near, passed, second_passed, sums, scale],
    )
    cols_one = jnp.sum(cols[:, 1], axis=0)
    next_log_scale = math.log(target) - jnp.log(cols_one)
    return rebuilt, next_log_scale


def solution(mesh):
    sizes = (RING, RING, RING, RING, 2)
    rings = jax.sharding.Mesh(mesh.devices.reshape(sizes), ("x", "z_hi", "y", "z_lo", "core"))
    block, book = P(ITEMS, None), P(CODES, ITEMS)
    return jax.shard_map(
        shards,
        mesh=rings,
        in_specs=(block, block, book, book),
        out_specs=(P(ITEMS, CODES), P(CODES)),
        check_vma=False,
    )
```

```python
import functools
import math

import jax
import jax.numpy as jnp
from jax import lax
from jax.experimental import pallas as pl
from jax.experimental.pallas import tpu as pltpu
from jax.sharding import PartitionSpec as P

SWEEPS = 3
RING = 4
PLANE = ("x", "y")
CODES = ("z_lo", "core")
ITEMS = ("x", "z_hi", "y")
MIB = 1 << 20
STEP = 256
MOST = 48 * MIB
HBM = pl.BlockSpec(memory_space=pltpu.HBM)
FULL = pl.BlockSpec(memory_space=pltpu.VMEM)
BF16 = jnp.bfloat16
F32 = jnp.float32


def call(body, outs, name, ins, flops=0, nbytes=4 * MIB, limit=16 * MIB, scratch=(), out_specs=None):
    ins = [i if isinstance(i, tuple) else (i, FULL) for i in ins]
    specs = {} if out_specs is None else {"out_specs": out_specs}
    return pl.pallas_call(
        body,
        out_shape=outs,
        in_specs=[spec for _, spec in ins],
        scratch_shapes=list(scratch),
        compiler_params=pltpu.CompilerParams(vmem_limit_bytes=limit),
        cost_estimate=pl.CostEstimate(flops=flops, bytes_accessed=nbytes, transcendentals=0),
        name=name,
        **specs,
    )(*[array for array, _ in ins])


def shape(*sizes, of=F32):
    return jax.ShapeDtypeStruct(sizes, of)


def spread(rows, count):
    return jnp.broadcast_to(rows[None], (count,) + rows.shape)


def nt(a, b):
    return lax.dot_general(a, b, (((1,), (1,)), ((), ())), preferred_element_type=F32)


def nn(a, b):
    return jnp.dot(a, b, preferred_element_type=F32)


def k_rows(block, book, norms, inv_root):
    scores = nn(block, book)
    return jnp.exp((scores - norms) * inv_root).astype(BF16)


def fan_body(copies, column, two, one):
    run = column.shape[1] // 2
    for z in range(column.shape[0]):
        one[z] = column[z, run:, :]
        for i in range(copies):
            two[i, z] = column[z, :run, :]


def fetch_book(came, book, sems):
    fetches = []
    for x in range(RING):
        for y in range(RING):
            move = pltpu.make_async_copy(came.at[x * RING + y], book.at[x, :, y], sems.at[x * RING + y])
            move.start()
            fetches.append(move)
    return fetches


def half_norms(book, fetches):
    acc = jnp.zeros(book.shape[3:], F32)
    for x in range(RING):
        for y in range(RING):
            fetches[x * RING + y].wait()
            for z in range(RING):
                wide = book[x, z, y].astype(F32)
                acc = acc + wide * wide
    return 0.5 * jnp.sum(acc, axis=0, keepdims=True)


def make_k(inv_root, groups, came, block, k, total, book, held, sems, after_step=None):
    rows, features = block.shape
    codes = book.shape[-1]
    fetches = fetch_book(came, book, sems)
    loads = []
    for i in range(rows // STEP):
        here = pl.ds(i * STEP, STEP)
        loads.append(pltpu.make_async_copy(block.at[here], held.at[here], sems.at[len(fetches) + i]))
        loads[-1].start()
    norms = half_norms(book, fetches)
    ones = jnp.ones((16, codes), BF16)
    for i, load in enumerate(loads):
        here = slice(i * STEP, (i + 1) * STEP)
        load.wait()
        values = k_rows(held[here, :], book[...].reshape(features, codes), norms, inv_root)
        k[here, :] = values
        total[:, :, here] = spread(nt(ones, values)[0:1], groups)
        if after_step is not None:
            after_step(i)


def kernel_two_body(inv_root, groups, came, block, k_out, total, book, held, sems):
    make_k(inv_root, groups, came, block, k_out, total, book, held, sems)


def kernel_one_body(inv_root, groups, came, block, after, k_out, total, book, held, k, sems, saved):
    saves = []

    def save(i):
        here = pl.ds(i * STEP, STEP)
        saves.append(pltpu.make_async_copy(k.at[here], k_out.at[here], saved.at[i]))
        saves[-1].start()

    make_k(inv_root, groups, came, block, k, total, book, held, sems, save)
    for move in saves:
        move.wait()


def two_terms(row):
    high = row.astype(BF16).astype(F32)
    at = lax.broadcasted_iota(jnp.int32, (16, row.shape[1]), 0)
    return jnp.where(at == 0, high, jnp.where(at == 1, row - high, 0.0)).astype(BF16)


def over_codes(scale, k):
    return jnp.sum(nt(two_terms(scale), k[...]), axis=0, keepdims=True)


def over_items(scale, k):
    return jnp.sum(nn(two_terms(scale), k[...]), axis=0, keepdims=True)


def col_body(copies, gathered, k, col_out, scale_out):
    scale = 1.0 / jnp.sum(gathered[...], axis=0)
    scale_out[...] = scale
    col_out[...] = spread(over_items(scale, k), copies)


def both_cols_body(copies, gathered, k, k_one, col_out, scale_out, held, sem):
    fetch = pltpu.make_async_copy(k_one, held, sem)
    fetch.start()
    scale = 1.0 / jnp.sum(gathered[...], axis=0)
    scale_out[...] = scale[0:1]
    col_out[:, 0:1, :] = spread(over_items(scale[0:1], k), copies)
    fetch.wait()
    col_out[:, 1:2, :] = spread(over_items(scale[1:2], held), copies)


def row_body(target, groups, cols, k, after, *refs):
    out = refs[-1]
    scale = target / jnp.sum(cols[...], axis=0)[0:1]
    out[:, 0:1, :] = spread(over_codes(scale, k), groups)
    for more in refs[:-1]:
        out[:, 1:2, :] = more[...]


def halves(row):
    high = row.astype(BF16)
    return high, (row - high.astype(F32)).astype(BF16)


def cut(row, width):
    return jnp.concatenate([row[:, i : i + width] for i in range(0, row.shape[1], width)], 0)


def turn_body(groups, came, after, out, book, sems):
    features, codes = out.shape[1], out.shape[0]
    for fetch in fetch_book(came, book, sems):
        fetch.wait()
    width = features // groups
    core = lax.axis_index("core")
    z_hi = width // (RING * book.shape[3])
    for mine in range(2):
        parity = core if mine else 1 - core
        for x in range(RING):
            to = (mine * RING + x) * width
            part = book[x, pl.ds(z_hi * parity, z_hi)].reshape(width, codes)
            out[:, to : to + width] = part.T


def transport_body(target, cols, r, k, turned, t_out, other_out, sums_out):
    rows = k.shape[0]
    wide = other_out.shape[1]
    scale = target / jnp.sum(cols[...], axis=0)[0:1]
    sums = over_codes(scale, k)
    sums_out[...] = sums
    parts = jnp.concatenate([cut(part.astype(F32), wide) for part in halves(sums)], 0)
    filled = jnp.concatenate([parts, jnp.zeros((16 - parts.shape[0], wide), F32)], 0)
    other_out[rows : rows + 16, :] = filled.astype(BF16)
    r_up = jnp.transpose(jnp.broadcast_to(r[0:1, :], (8, r.shape[1])))
    for i in range(rows // STEP):
        here = slice(i * STEP, (i + 1) * STEP)
        t = (r_up[here, 0:1] * k[here, :].astype(F32) * scale).astype(BF16)
        t_out[here, :] = t
        other_out[here, :] = nn(t, turned[:, :wide]).astype(BF16)


def mine_body(t, turned, out):
    wide = out.shape[1]
    for i in range(t.shape[0] // STEP):
        here = slice(i * STEP, (i + 1) * STEP)
        out[here, :] = nn(t[here, :], turned[:, wide:])


def pack(sums):
    return jnp.concatenate([part.astype(F32) for part in halves(sums)], 0).astype(BF16)


def unpack(tail):
    tail = tail.astype(F32)
    return tail[:8] + tail[8:]


def pair_body(mine, came, sums, here_out, far_out, sums_out, cross_out, beside_out):
    rows, wide = mine.shape
    width = wide // RING
    tail = came[rows : rows + 16, :].astype(F32)
    n = rows // wide
    theirs = [tail[i : i + 1, :] + tail[n + i : n + i + 1, :] for i in range(n)]
    both = cut(sums[...] + jnp.concatenate(theirs, 1), width)
    sums_out[...] = both
    z = lax.axis_index("z_lo")
    pair = z + 1 - 2 * (z % 2)
    far = (z + 2) % RING
    for chip, out in ((z, here_out), (far, far_out), ((pair + 2) % RING, cross_out), (pair, beside_out)):
        lanes = pl.ds(pl.multiple_of(chip * width, width), width)
        value = mine[:, lanes] + came[:rows, lanes].astype(F32)
        out[:rows, :] = value.astype(out.dtype)
    cross_out[rows : rows + 16, :] = pack(both)


def cross_body(far, came, sums, out, sums_out):
    rows = far.shape[0]
    out[:rows, :] = (far[...] + came[:rows, :].astype(F32)).astype(BF16)
    both = sums[...] + unpack(came[rows : rows + 16, :])
    sums_out[...] = both
    out[rows : rows + 16, :] = pack(both)


def last_body(own, beside, far, sums, r, out):
    rows, width = out.shape
    total = sums[...] + unpack(far[rows : rows + 16, :])
    ratio = jnp.transpose(1.0 / (cut(r[0:1, :], width) * total))
    for i in range(rows // width):
        here = slice(i * width, (i + 1) * width)
        value = own[here, :] + beside[here, :].astype(F32) + far[here, :].astype(F32)
        out[here, :] = (value * ratio[:, i : i + 1]).astype(out.dtype)


def shards(block_two, block_one, codebook_two, codebook_one):
    rows, features = block_two.shape
    codes, run = codebook_two.shape
    groups = lax.axis_size(CODES)
    target = float(rows * lax.axis_size(ITEMS)) / float(codes * groups)
    inv_root = 1.0 / math.sqrt(features)
    book_flops = 2 * rows * features * codes

    plane = RING * RING
    sem = pltpu.SemaphoreType.DMA
    steps = rows // STEP
    both_books = spread(jnp.concatenate([codebook_two.T, codebook_one.T], 0), RING)
    column = lax.all_to_all(both_books, "z_hi", 0, 0)
    two, one = call(
        functools.partial(fan_body, plane),
        (shape(plane, RING, run, codes, of=BF16), shape(RING, run, codes, of=BF16)),
        "fan",
        [column],
    )
    came_two = lax.all_to_all(two, PLANE, 0, 0)
    came_two, one = lax.optimization_barrier((came_two, one))
    came_one = lax.all_gather(one, PLANE, axis=0, tiled=False)
    book_room = [
        pltpu.VMEM((RING, RING, RING, run, codes), BF16),
        pltpu.VMEM((rows, features), BF16),
    ]
    k_two, row_sums = call(
        functools.partial(kernel_two_body, inv_root, groups),
        (shape(rows, codes, of=BF16), shape(groups, 1, rows)),
        "kernel_two",
        [(came_two, HBM), (block_two, HBM)],
        flops=book_flops,
        limit=MOST + 4 * MIB - MIB // 4,
        scratch=book_room + [sem((plane + steps,))],
    )

    def make_k_one(after):
        return call(
            functools.partial(kernel_one_body, inv_root, groups),
            (shape(rows, codes, of=BF16), shape(groups, 1, rows)),
            "kernel_one",
            [(came_one, HBM), (block_one, HBM), (after, HBM)],
            flops=book_flops,
            limit=MOST + 4 * MIB - MIB // 4,
            scratch=book_room + [pltpu.VMEM((rows, codes), BF16), sem((plane + steps,)), sem((steps,))],
            out_specs=(HBM, FULL),
        )

    more, turned = [], k_two
    small = 32 * rows * codes
    for sweep in range(SWEEPS):
        last = sweep == SWEEPS - 1
        n = 2 if last else 1
        gathered = lax.all_to_all(row_sums, CODES, 0, 0)
        outs = (shape(plane, n, codes), shape(1, rows))
        if last:
            col, scale = call(
                functools.partial(both_cols_body, plane),
                outs,
                "columns",
                [gathered, k_two, (k_one, HBM)],
                flops=small,
                limit=MOST,
                scratch=[pltpu.VMEM((rows, codes), BF16), sem],
            )
        else:
            col, scale = call(
                functools.partial(col_body, plane), outs, "columns", [gathered, k_two], flops=small
            )
        col = spread(jnp.sum(lax.all_to_all(col, PLANE, 0, 0), axis=0), RING)
        cols = lax.all_to_all(col, "z_hi", 0, 0)
        if sweep == 1:
            k_one, first_one = make_k_one(col)
            turned = call(
                functools.partial(turn_body, groups),
                shape(codes, features, of=BF16),
                "turn",
                [(came_two, HBM), (first_one, HBM)],
                limit=MOST + 2 * MIB,
                scratch=[book_room[0], sem((plane,))],
            )
            more = [first_one]
        if not last:
            row_sums = call(
                functools.partial(row_body, target, groups),
                shape(groups, 1 + len(more), rows),
                "rows",
                [cols, k_two, (turned, HBM)] + more,
                flops=small,
            )

    wide = features // 2
    width = features // groups
    t, other, sums = call(
        functools.partial(transport_body, target),
        (shape(rows, codes, of=BF16), shape(rows + 16, wide, of=BF16), shape(1, rows)),
        "transport",
        [cols, scale, k_two, turned],
        flops=book_flops // 2,
        limit=24 * MIB,
    )
    came = lax.ppermute(other, "core", [(0, 1), (1, 0)])
    mine = call(
        mine_body, shape(rows, wide), "mine", [t, turned], flops=book_flops // 2, limit=24 * MIB
    )
    tall = shape(rows + 16, width, of=BF16)
    own, far, sums, cross, beside = call(
        pair_body,
        (shape(rows, width), shape(rows, width), shape(8, width), tall, shape(rows, width, of=BF16)),
        "pair",
        [mine, came, sums],
        limit=24 * MIB,
    )
    neighbours = [(0, 1), (1, 0), (2, 3), (3, 2)]
    crossed = lax.ppermute(cross, "z_lo", neighbours)
    beside = lax.ppermute(beside, "z_lo", neighbours)
    passed, sums = call(cross_body, (tall, shape(8, width)), "cross", [far, crossed, sums])
    passed = lax.ppermute(passed, "z_lo", [(0, 2), (2, 0), (1, 3), (3, 1)])
    rebuilt = call(
        last_body, shape(rows, width, of=BF16), "last", [own, beside, passed, sums, scale]
    )
    cols_one = jnp.sum(cols[:, 1], axis=0)
    next_log_scale = math.log(target) - jnp.log(cols_one)
    return rebuilt, next_log_scale


def solution(mesh):
    sizes = (RING, RING, RING, RING, 2)
    rings = jax.sharding.Mesh(mesh.devices.reshape(sizes), ("x", "z_hi", "y", "z_lo", "core"))
    block, book = P(ITEMS, None), P(CODES, ITEMS)
    return jax.shard_map(
        shards,
        mesh=rings,
        in_specs=(block, block, book, book),
        out_specs=(P(ITEMS, CODES), P(CODES)),
        check_vma=False,
    )
```

```python
import functools
import math

import jax
import jax.numpy as jnp
from jax import lax
from jax.experimental import pallas as pl
from jax.experimental.pallas import tpu as pltpu
from jax.sharding import PartitionSpec as P

SWEEPS = 3
RING = 4
PLANE = ("x", "y")
CODES = ("z_lo", "core")
ITEMS = ("x", "z_hi", "y")
MIB = 1 << 20
STEP = 256
MOST = 48 * MIB
HBM = pl.BlockSpec(memory_space=pltpu.HBM)
FULL = pl.BlockSpec(memory_space=pltpu.VMEM)
BF16 = jnp.bfloat16
F32 = jnp.float32


def call(body, outs, name, ins, flops=0, nbytes=4 * MIB, limit=16 * MIB, scratch=(), out_specs=None):
    ins = [i if isinstance(i, tuple) else (i, FULL) for i in ins]
    specs = {} if out_specs is None else {"out_specs": out_specs}
    return pl.pallas_call(
        body,
        out_shape=outs,
        in_specs=[spec for _, spec in ins],
        scratch_shapes=list(scratch),
        compiler_params=pltpu.CompilerParams(vmem_limit_bytes=limit),
        cost_estimate=pl.CostEstimate(flops=flops, bytes_accessed=nbytes, transcendentals=0),
        name=name,
        **specs,
    )(*[array for array, _ in ins])


def shape(*sizes, of=F32):
    return jax.ShapeDtypeStruct(sizes, of)


def spread(rows, count):
    return jnp.broadcast_to(rows[None], (count,) + rows.shape)


def nt(a, b):
    return lax.dot_general(a, b, (((1,), (1,)), ((), ())), preferred_element_type=F32)


def nn(a, b):
    return jnp.dot(a, b, preferred_element_type=F32)


def k_rows(block, book, norms, inv_root):
    scores = nn(block, book)
    return jnp.exp((scores - norms) * inv_root).astype(BF16)


def fan_body(copies, column, two, one):
    run = column.shape[1] // 2
    for z in range(column.shape[0]):
        one[z] = column[z, run:, :]
        for i in range(copies):
            two[i, z] = column[z, :run, :]


def fetch_book(came, book, sems):
    fetches = []
    for x in range(RING):
        for y in range(RING):
            move = pltpu.make_async_copy(came.at[x * RING + y], book.at[x, :, y], sems.at[x * RING + y])
            move.start()
            fetches.append(move)
    return fetches


def half_norms(book, fetches):
    acc = jnp.zeros(book.shape[3:], F32)
    for x in range(RING):
        for y in range(RING):
            fetches[x * RING + y].wait()
            for z in range(RING):
                wide = book[x, z, y].astype(F32)
                acc = acc + wide * wide
    return 0.5 * jnp.sum(acc, axis=0, keepdims=True)


def make_k(inv_root, groups, came, block, k, total, book, held, sems, after_step=None):
    rows, features = block.shape
    codes = book.shape[-1]
    fetches = fetch_book(came, book, sems)
    loads = []
    for i in range(rows // STEP):
        here = pl.ds(i * STEP, STEP)
        loads.append(pltpu.make_async_copy(block.at[here], held.at[here], sems.at[len(fetches) + i]))
        loads[-1].start()
    norms = half_norms(book, fetches)
    ones = jnp.ones((16, codes), BF16)
    for i, load in enumerate(loads):
        here = slice(i * STEP, (i + 1) * STEP)
        load.wait()
        values = k_rows(held[here, :], book[...].reshape(features, codes), norms, inv_root)
        k[here, :] = values
        total[:, :, here] = spread(nt(ones, values)[0:1], groups)
        if after_step is not None:
            after_step(i)


def kernel_two_body(inv_root, groups, came, block, k_out, total, book, held, sems):
    make_k(inv_root, groups, came, block, k_out, total, book, held, sems)


def kernel_one_body(inv_root, groups, came, block, after, k_out, total, book, held, k, sems, saved):
    saves = []

    def save(i):
        here = pl.ds(i * STEP, STEP)
        saves.append(pltpu.make_async_copy(k.at[here], k_out.at[here], saved.at[i]))
        saves[-1].start()

    make_k(inv_root, groups, came, block, k, total, book, held, sems, save)
    for move in saves:
        move.wait()


def two_terms(row):
    high = row.astype(BF16).astype(F32)
    at = lax.broadcasted_iota(jnp.int32, (16, row.shape[1]), 0)
    return jnp.where(at == 0, high, jnp.where(at == 1, row - high, 0.0)).astype(BF16)


def over_codes(scale, k):
    return jnp.sum(nt(two_terms(scale), k[...]), axis=0, keepdims=True)


def over_items(scale, k):
    return jnp.sum(nn(two_terms(scale), k[...]), axis=0, keepdims=True)


def col_body(copies, gathered, k, col_out, scale_out):
    scale = 1.0 / jnp.sum(gathered[...], axis=0)
    scale_out[...] = scale
    col_out[...] = spread(over_items(scale, k), copies)


def both_cols_body(copies, gathered, k, k_one, came, col_out, scale_out, theirs, ours, held, sem, sems, our_sems):
    core = lax.axis_index("core")
    fetch = pltpu.make_async_copy(k_one, held, sem)
    fetch.start()
    picks = fetch_parity(came, theirs, 1 - core, sems) + fetch_parity(came, ours, core, our_sems)
    scale = 1.0 / jnp.sum(gathered[...], axis=0)
    scale_out[...] = scale[0:1]
    col_out[:, 0:1, :] = spread(over_items(scale[0:1], k), copies)
    fetch.wait()
    col_out[:, 1:2, :] = spread(over_items(scale[1:2], held), copies)
    for pick in picks:
        pick.wait()


def row_body(target, groups, cols, k, *refs):
    out = refs[-1]
    scale = target / jnp.sum(cols[...], axis=0)[0:1]
    out[:, 0:1, :] = spread(over_codes(scale, k), groups)
    for more in refs[:-1]:
        out[:, 1:2, :] = more[...]


def halves(row):
    high = row.astype(BF16)
    return high, (row - high.astype(F32)).astype(BF16)


def cut(row, width):
    return jnp.concatenate([row[:, i : i + width] for i in range(0, row.shape[1], width)], 0)


def fetch_parity(came, picked, parity, sems):
    fetches = []
    for x in range(RING):
        for y in range(RING):
            here = came.at[x * RING + y, pl.ds(2 * parity, 2)]
            move = pltpu.make_async_copy(here, picked.at[x, :, y], sems.at[x * RING + y])
            move.start()
            fetches.append(move)
    return fetches


def transport_body(target, cols, r, k, theirs, t_out, other_out, sums_out):
    rows, codes = k.shape
    wide = other_out.shape[1]
    scale = target / jnp.sum(cols[...], axis=0)[0:1]
    sums = over_codes(scale, k)
    sums_out[...] = sums
    parts = jnp.concatenate([cut(part.astype(F32), wide) for part in halves(sums)], 0)
    filled = jnp.concatenate([parts, jnp.zeros((16 - parts.shape[0], wide), F32)], 0)
    other_out[rows : rows + 16, :] = filled.astype(BF16)
    r_up = jnp.transpose(jnp.broadcast_to(r[0:1, :], (8, r.shape[1])))
    for i in range(rows // STEP):
        here = slice(i * STEP, (i + 1) * STEP)
        t = (r_up[here, 0:1] * k[here, :].astype(F32) * scale).astype(BF16)
        t_out[here, :] = t
        other_out[here, :] = nt(t, theirs[...].reshape(wide, codes)).astype(BF16)


def mine_body(t, ours, out):
    wide = out.shape[1]
    for i in range(t.shape[0] // STEP):
        here = slice(i * STEP, (i + 1) * STEP)
        out[here, :] = nt(t[here, :], ours[...].reshape(wide, t.shape[1]))


def pack(sums):
    return jnp.concatenate([part.astype(F32) for part in halves(sums)], 0).astype(BF16)


def unpack(tail):
    tail = tail.astype(F32)
    return tail[:8] + tail[8:]


def pair_body(mine, came, sums, here_out, far_out, sums_out, cross_out, beside_out):
    rows, wide = mine.shape
    width = wide // RING
    tail = came[rows : rows + 16, :].astype(F32)
    n = rows // wide
    theirs = [tail[i : i + 1, :] + tail[n + i : n + i + 1, :] for i in range(n)]
    both = cut(sums[...] + jnp.concatenate(theirs, 1), width)
    sums_out[...] = both
    z = lax.axis_index("z_lo")
    pair = z + 1 - 2 * (z % 2)
    far = (z + 2) % RING
    for chip, out in ((z, here_out), (far, far_out), ((pair + 2) % RING, cross_out), (pair, beside_out)):
        lanes = pl.ds(pl.multiple_of(chip * width, width), width)
        value = mine[:, lanes] + came[:rows, lanes].astype(F32)
        out[:rows, :] = value.astype(out.dtype)
    cross_out[rows : rows + 16, :] = pack(both)


def cross_body(far, came, sums, out, sums_out):
    rows = far.shape[0]
    out[:rows, :] = (far[...] + came[:rows, :].astype(F32)).astype(BF16)
    both = sums[...] + unpack(came[rows : rows + 16, :])
    sums_out[...] = both
    out[rows : rows + 16, :] = pack(both)


def last_body(own, beside, far, sums, r, out):
    rows, width = out.shape
    total = sums[...] + unpack(far[rows : rows + 16, :])
    ratio = jnp.transpose(1.0 / (cut(r[0:1, :], width) * total))
    for i in range(rows // width):
        here = slice(i * width, (i + 1) * width)
        value = own[here, :] + beside[here, :].astype(F32) + far[here, :].astype(F32)
        out[here, :] = (value * ratio[:, i : i + 1]).astype(out.dtype)


def shards(block_two, block_one, codebook_two, codebook_one):
    rows, features = block_two.shape
    codes, run = codebook_two.shape
    groups = lax.axis_size(CODES)
    target = float(rows * lax.axis_size(ITEMS)) / float(codes * groups)
    inv_root = 1.0 / math.sqrt(features)
    book_flops = 2 * rows * features * codes

    plane = RING * RING
    sem = pltpu.SemaphoreType.DMA
    steps = rows // STEP
    both_books = spread(jnp.concatenate([codebook_two.T, codebook_one.T], 0), RING)
    column = lax.all_to_all(both_books, "z_hi", 0, 0)
    two, one = call(
        functools.partial(fan_body, plane),
        (shape(plane, RING, run, codes, of=BF16), shape(RING, run, codes, of=BF16)),
        "fan",
        [column],
    )
    came_two = lax.all_to_all(two, PLANE, 0, 0)
    came_two, one = lax.optimization_barrier((came_two, one))
    came_one = lax.all_gather(one, PLANE, axis=0, tiled=False)
    book_room = [
        pltpu.VMEM((RING, RING, RING, run, codes), BF16),
        pltpu.VMEM((rows, features), BF16),
    ]
    k_two, row_sums = call(
        functools.partial(kernel_two_body, inv_root, groups),
        (shape(rows, codes, of=BF16), shape(groups, 1, rows)),
        "kernel_two",
        [(came_two, HBM), (block_two, HBM)],
        flops=book_flops,
        limit=MOST + 4 * MIB - MIB // 4,
        scratch=book_room + [sem((plane + steps,))],
    )

    def make_k_one(after):
        return call(
            functools.partial(kernel_one_body, inv_root, groups),
            (shape(rows, codes, of=BF16), shape(groups, 1, rows)),
            "kernel_one",
            [(came_one, HBM), (block_one, HBM), (after, HBM)],
            flops=book_flops,
            limit=MOST + 2 * MIB,
            scratch=book_room + [pltpu.VMEM((rows, codes), BF16), sem((plane + steps,)), sem((steps,))],
            out_specs=(HBM, FULL),
        )

    more = []
    small = 32 * rows * codes
    for sweep in range(SWEEPS):
        last = sweep == SWEEPS - 1
        n = 2 if last else 1
        gathered = lax.all_to_all(row_sums, CODES, 0, 0)
        outs = (shape(plane, n, codes), shape(1, rows))
        if last:
            parity = shape(RING, 2, RING, run, codes, of=BF16)
            col, scale, theirs, ours = call(
                functools.partial(both_cols_body, plane),
                outs + (parity, parity),
                "columns",
                [gathered, k_two, (k_one, HBM), (came_two, HBM)],
                flops=small,
                limit=MOST,
                scratch=[pltpu.VMEM((rows, codes), BF16), sem, sem((plane,)), sem((plane,))],
            )
        else:
            col, scale = call(
                functools.partial(col_body, plane), outs, "columns", [gathered, k_two], flops=small
            )
        col = spread(jnp.sum(lax.all_to_all(col, PLANE, 0, 0), axis=0), RING)
        cols = lax.all_to_all(col, "z_hi", 0, 0)
        if sweep == 1:
            k_one, first_one = make_k_one(col)
            more = [first_one]
        if not last:
            row_sums = call(
                functools.partial(row_body, target, groups),
                shape(groups, 1 + len(more), rows),
                "rows",
                [cols, k_two] + more,
                flops=small,
            )

    wide = features // 2
    width = features // groups
    t, other, sums = call(
        functools.partial(transport_body, target),
        (shape(rows, codes, of=BF16), shape(rows + 16, wide, of=BF16), shape(1, rows)),
        "transport",
        [cols, scale, k_two, theirs],
        flops=book_flops // 2,
        limit=24 * MIB,
    )
    came = lax.ppermute(other, "core", [(0, 1), (1, 0)])
    mine = call(
        mine_body, shape(rows, wide), "mine", [t, ours], flops=book_flops // 2, limit=24 * MIB
    )
    tall = shape(rows + 16, width, of=BF16)
    own, far, sums, cross, beside = call(
        pair_body,
        (shape(rows, width), shape(rows, width), shape(8, width), tall, shape(rows, width, of=BF16)),
        "pair",
        [mine, came, sums],
        limit=24 * MIB,
    )
    neighbours = [(0, 1), (1, 0), (2, 3), (3, 2)]
    crossed = lax.ppermute(cross, "z_lo", neighbours)
    beside = lax.ppermute(beside, "z_lo", neighbours)
    passed, sums = call(cross_body, (tall, shape(8, width)), "cross", [far, crossed, sums])
    passed = lax.ppermute(passed, "z_lo", [(0, 2), (2, 0), (1, 3), (3, 1)])
    rebuilt = call(
        last_body, shape(rows, width, of=BF16), "last", [own, beside, passed, sums, scale]
    )
    cols_one = jnp.sum(cols[:, 1], axis=0)
    next_log_scale = math.log(target) - jnp.log(cols_one)
    return rebuilt, next_log_scale


def solution(mesh):
    sizes = (RING, RING, RING, RING, 2)
    rings = jax.sharding.Mesh(mesh.devices.reshape(sizes), ("x", "z_hi", "y", "z_lo", "core"))
    block, book = P(ITEMS, None), P(CODES, ITEMS)
    return jax.shard_map(
        shards,
        mesh=rings,
        in_specs=(block, block, book, book),
        out_specs=(P(ITEMS, CODES), P(CODES)),
        check_vma=False,
    )
```

```python
import functools
import math

import jax
import jax.numpy as jnp
from jax import lax
from jax.experimental import pallas as pl
from jax.experimental.pallas import tpu as pltpu
from jax.sharding import PartitionSpec as P

SWEEPS = 3
RING = 4
PLANE = ("x", "y")
CODES = ("z_lo", "core")
ITEMS = ("x", "z_hi", "y")
MIB = 1 << 20
STEP = 256
MOST = 48 * MIB
HBM = pl.BlockSpec(memory_space=pltpu.HBM)
FULL = pl.BlockSpec(memory_space=pltpu.VMEM)
BF16 = jnp.bfloat16
F32 = jnp.float32


def call(body, outs, name, ins, flops=0, nbytes=4 * MIB, limit=16 * MIB, scratch=(), out_specs=None):
    ins = [i if isinstance(i, tuple) else (i, FULL) for i in ins]
    specs = {} if out_specs is None else {"out_specs": out_specs}
    return pl.pallas_call(
        body,
        out_shape=outs,
        in_specs=[spec for _, spec in ins],
        scratch_shapes=list(scratch),
        compiler_params=pltpu.CompilerParams(vmem_limit_bytes=limit),
        cost_estimate=pl.CostEstimate(flops=flops, bytes_accessed=nbytes, transcendentals=0),
        name=name,
        **specs,
    )(*[array for array, _ in ins])


def shape(*sizes, of=F32):
    return jax.ShapeDtypeStruct(sizes, of)


def spread(rows, count):
    return jnp.broadcast_to(rows[None], (count,) + rows.shape)


def nt(a, b):
    return lax.dot_general(a, b, (((1,), (1,)), ((), ())), preferred_element_type=F32)


def nn(a, b):
    return jnp.dot(a, b, preferred_element_type=F32)


def k_rows(block, book, norms, inv_root):
    scores = nn(block, book)
    return jnp.exp((scores - norms) * inv_root).astype(BF16)


def fan_body(copies, column, two, one):
    run = column.shape[1] // 2
    for z in range(column.shape[0]):
        one[z] = column[z, run:, :]
        for i in range(copies):
            two[i, z] = column[z, :run, :]


def fetch_book(came, book, sems):
    fetches = []
    for x in range(RING):
        for y in range(RING):
            move = pltpu.make_async_copy(came.at[x * RING + y], book.at[x, :, y], sems.at[x * RING + y])
            move.start()
            fetches.append(move)
    return fetches


def half_norms(book, fetches):
    acc = jnp.zeros(book.shape[3:], F32)
    for x in range(RING):
        for y in range(RING):
            fetches[x * RING + y].wait()
            for z in range(RING):
                wide = book[x, z, y].astype(F32)
                acc = acc + wide * wide
    return 0.5 * jnp.sum(acc, axis=0, keepdims=True)


def make_k(inv_root, groups, start, came, block, k, total, book, held, sems, after_step=None):
    rows, features = held.shape
    codes = book.shape[-1]
    fetches = fetch_book(came, book, sems)
    loads = []
    for i in range(rows // STEP):
        here = pl.ds(i * STEP, STEP)
        there = pl.ds(start + i * STEP, STEP)
        loads.append(pltpu.make_async_copy(block.at[there], held.at[here], sems.at[len(fetches) + i]))
        loads[-1].start()
    norms = half_norms(book, fetches)
    ones = jnp.ones((16, codes), BF16)
    for i, load in enumerate(loads):
        here = slice(i * STEP, (i + 1) * STEP)
        load.wait()
        values = k_rows(held[here, :], book[...].reshape(features, codes), norms, inv_root)
        k[here, :] = values
        total[:, :, here] = spread(nt(ones, values)[0:1], groups)
        if after_step is not None:
            after_step(i)


def kernel_two_body(inv_root, groups, came, block, k_out, total, book, held, sems):
    make_k(inv_root, groups, 0, came, block, k_out, total, book, held, sems)


def kernel_one_body(inv_root, groups, start, came, block, after, k_out, total, book, held, k, sems, saved):
    saves = []

    def save(i):
        here = pl.ds(i * STEP, STEP)
        saves.append(pltpu.make_async_copy(k.at[here], k_out.at[here], saved.at[i]))
        saves[-1].start()

    make_k(inv_root, groups, start, came, block, k, total, book, held, sems, save)
    for move in saves:
        move.wait()


def two_terms(row):
    high = row.astype(BF16).astype(F32)
    at = lax.broadcasted_iota(jnp.int32, (16, row.shape[1]), 0)
    return jnp.where(at == 0, high, jnp.where(at == 1, row - high, 0.0)).astype(BF16)


def over_codes(scale, k):
    return jnp.sum(nt(two_terms(scale), k[...]), axis=0, keepdims=True)


def over_items(scale, k):
    return jnp.sum(nn(two_terms(scale), k[...]), axis=0, keepdims=True)


def col_body(copies, gathered, k, col_out, scale_out):
    scale = 1.0 / jnp.sum(gathered[...], axis=0)
    scale_out[...] = scale
    col_out[...] = spread(over_items(scale, k), copies)


def both_cols_body(copies, gathered, k, first, second, col_out, scale_out, held, sems):
    half = first.shape[0]
    fetches = []
    for i, part in enumerate((first, second)):
        fetches.append(pltpu.make_async_copy(part, held.at[pl.ds(i * half, half)], sems.at[i]))
        fetches[-1].start()
    scale = 1.0 / jnp.sum(gathered[...], axis=0)
    scale_out[...] = scale[0:1]
    col_out[:, 0:1, :] = spread(over_items(scale[0:1], k), copies)
    for fetch in fetches:
        fetch.wait()
    col_out[:, 1:2, :] = spread(over_items(scale[1:2], held), copies)


def row_body(target, groups, cols, k, *refs):
    out = refs[-1]
    scale = target / jnp.sum(cols[...], axis=0)[0:1]
    out[:, 0:1, :] = spread(over_codes(scale, k), groups)
    at = 0
    for more in refs[:-1]:
        out[:, 1:2, at : at + more.shape[2]] = more[...]
        at += more.shape[2]


def halves(row):
    high = row.astype(BF16)
    return high, (row - high.astype(F32)).astype(BF16)


def cut(row, width):
    return jnp.concatenate([row[:, i : i + width] for i in range(0, row.shape[1], width)], 0)


def pick(came, picked, parity):
    for x in range(RING):
        for y in range(RING):
            for z in range(2):
                picked[x, z, y] = came[x * RING + y, 2 * parity + z]


def transport_body(target, cols, r, k, came, t_out, other_out, sums_out, picked):
    rows, codes = k.shape
    wide = other_out.shape[1]
    scale = target / jnp.sum(cols[...], axis=0)[0:1]
    sums = over_codes(scale, k)
    sums_out[...] = sums
    pick(came, picked, 1 - lax.axis_index("core"))
    parts = jnp.concatenate([cut(part.astype(F32), wide) for part in halves(sums)], 0)
    filled = jnp.concatenate([parts, jnp.zeros((16 - parts.shape[0], wide), F32)], 0)
    other_out[rows : rows + 16, :] = filled.astype(BF16)
    r_up = jnp.transpose(jnp.broadcast_to(r[0:1, :], (8, r.shape[1])))
    for i in range(rows // STEP):
        here = slice(i * STEP, (i + 1) * STEP)
        t = (r_up[here, 0:1] * k[here, :].astype(F32) * scale).astype(BF16)
        t_out[here, :] = t
        other_out[here, :] = nt(t, picked[...].reshape(wide, codes)).astype(BF16)


def mine_body(t, came, out, picked):
    wide = out.shape[1]
    pick(came, picked, lax.axis_index("core"))
    for i in range(t.shape[0] // STEP):
        here = slice(i * STEP, (i + 1) * STEP)
        out[here, :] = nt(t[here, :], picked[...].reshape(wide, t.shape[1]))


def pack(sums):
    return jnp.concatenate([part.astype(F32) for part in halves(sums)], 0).astype(BF16)


def unpack(tail):
    tail = tail.astype(F32)
    return tail[:8] + tail[8:]


def pair_body(mine, came, sums, here_out, far_out, sums_out, cross_out, beside_out):
    rows, wide = mine.shape
    width = wide // RING
    tail = came[rows : rows + 16, :].astype(F32)
    n = rows // wide
    theirs = [tail[i : i + 1, :] + tail[n + i : n + i + 1, :] for i in range(n)]
    both = cut(sums[...] + jnp.concatenate(theirs, 1), width)
    sums_out[...] = both
    z = lax.axis_index("z_lo")
    pair = z + 1 - 2 * (z % 2)
    far = (z + 2) % RING
    for chip, out in ((z, here_out), (far, far_out), ((pair + 2) % RING, cross_out), (pair, beside_out)):
        lanes = pl.ds(pl.multiple_of(chip * width, width), width)
        value = mine[:, lanes] + came[:rows, lanes].astype(F32)
        out[:rows, :] = value.astype(out.dtype)
    cross_out[rows : rows + 16, :] = pack(both)


def cross_body(far, came, sums, out, sums_out):
    rows = far.shape[0]
    out[:rows, :] = (far[...] + came[:rows, :].astype(F32)).astype(BF16)
    both = sums[...] + unpack(came[rows : rows + 16, :])
    sums_out[...] = both
    out[rows : rows + 16, :] = pack(both)


def last_body(own, beside, far, sums, r, out):
    rows, width = out.shape
    total = sums[...] + unpack(far[rows : rows + 16, :])
    ratio = jnp.transpose(1.0 / (cut(r[0:1, :], width) * total))
    for i in range(rows // width):
        here = slice(i * width, (i + 1) * width)
        value = own[here, :] + beside[here, :].astype(F32) + far[here, :].astype(F32)
        out[here, :] = (value * ratio[:, i : i + 1]).astype(out.dtype)


def shards(block_two, block_one, codebook_two, codebook_one):
    rows, features = block_two.shape
    codes, run = codebook_two.shape
    groups = lax.axis_size(CODES)
    target = float(rows * lax.axis_size(ITEMS)) / float(codes * groups)
    inv_root = 1.0 / math.sqrt(features)
    book_flops = 2 * rows * features * codes

    plane = RING * RING
    sem = pltpu.SemaphoreType.DMA
    steps = rows // STEP
    both_books = spread(jnp.concatenate([codebook_two.T, codebook_one.T], 0), RING)
    column = lax.all_to_all(both_books, "z_hi", 0, 0)
    two, one = call(
        functools.partial(fan_body, plane),
        (shape(plane, RING, run, codes, of=BF16), shape(RING, run, codes, of=BF16)),
        "fan",
        [column],
    )
    came_two = lax.all_to_all(two, PLANE, 0, 0)
    came_two, one = lax.optimization_barrier((came_two, one))
    came_one = lax.all_gather(one, PLANE, axis=0, tiled=False)
    book_room = [
        pltpu.VMEM((RING, RING, RING, run, codes), BF16),
        pltpu.VMEM((rows, features), BF16),
    ]
    k_two, row_sums = call(
        functools.partial(kernel_two_body, inv_root, groups),
        (shape(rows, codes, of=BF16), shape(groups, 1, rows)),
        "kernel_two",
        [(came_two, HBM), (block_two, HBM)],
        flops=book_flops,
        limit=MOST + 4 * MIB - MIB // 4,
        scratch=book_room + [sem((plane + steps,))],
    )

    half = rows // 2

    def make_k_one(start, after):
        return call(
            functools.partial(kernel_one_body, inv_root, groups, start),
            (shape(half, codes, of=BF16), shape(groups, 1, half)),
            "kernel_one",
            [(came_one, HBM), (block_one, HBM), (after, HBM)],
            flops=book_flops // 2,
            limit=MOST + 4 * MIB,
            scratch=[
                book_room[0],
                pltpu.VMEM((half, features), BF16),
                pltpu.VMEM((half, codes), BF16),
                sem((plane + steps // 2,)),
                sem((steps // 2,)),
            ],
            out_specs=(HBM, FULL),
        )

    more = []
    small = 32 * rows * codes
    for sweep in range(SWEEPS):
        last = sweep == SWEEPS - 1
        n = 2 if last else 1
        gathered = lax.all_to_all(row_sums, CODES, 0, 0)
        outs = (shape(plane, n, codes), shape(1, rows))
        if last:
            col, scale = call(
                functools.partial(both_cols_body, plane),
                outs,
                "columns",
                [gathered, k_two] + [(part, HBM) for part in k_one],
                flops=small,
                limit=MOST,
                scratch=[pltpu.VMEM((rows, codes), BF16), sem((2,))],
            )
        else:
            col, scale = call(
                functools.partial(col_body, plane), outs, "columns", [gathered, k_two], flops=small
            )
        col_all = lax.all_to_all(col, PLANE, 0, 0)
        if sweep == 1:
            first_k, first_one = make_k_one(0, col)
            col_all, first_one = lax.optimization_barrier((col_all, first_one))
        col = spread(jnp.sum(col_all, axis=0), RING)
        cols = lax.all_to_all(col, "z_hi", 0, 0)
        if sweep == 1:
            second_k, second_one = make_k_one(half, col)
            k_one, more = [first_k, second_k], [first_one, second_one]
        if not last:
            row_sums = call(
                functools.partial(row_body, target, groups),
                shape(groups, 2 if more else 1, rows),
                "rows",
                [cols, k_two] + more,
                flops=small,
            )

    wide = features // 2
    width = features // groups
    t, other, sums = call(
        functools.partial(transport_body, target),
        (shape(rows, codes, of=BF16), shape(rows + 16, wide, of=BF16), shape(1, rows)),
        "transport",
        [cols, scale, k_two, came_two],
        flops=book_flops // 2,
        limit=24 * MIB,
        scratch=[pltpu.VMEM((RING, 2, RING, run, codes), BF16)],
    )
    came = lax.ppermute(other, "core", [(0, 1), (1, 0)])
    mine = call(
        mine_body,
        shape(rows, wide),
        "mine",
        [t, came_two],
        flops=book_flops // 2,
        limit=24 * MIB,
        scratch=[pltpu.VMEM((RING, 2, RING, run, codes), BF16)],
    )
    tall = shape(rows + 16, width, of=BF16)
    own, far, sums, cross, beside = call(
        pair_body,
        (shape(rows, width), shape(rows, width), shape(8, width), tall, shape(rows, width, of=BF16)),
        "pair",
        [mine, came, sums],
        limit=24 * MIB,
    )
    neighbours = [(0, 1), (1, 0), (2, 3), (3, 2)]
    crossed = lax.ppermute(cross, "z_lo", neighbours)
    beside = lax.ppermute(beside, "z_lo", neighbours)
    passed, sums = call(cross_body, (tall, shape(8, width)), "cross", [far, crossed, sums])
    passed = lax.ppermute(passed, "z_lo", [(0, 2), (2, 0), (1, 3), (3, 1)])
    rebuilt = call(
        last_body, shape(rows, width, of=BF16), "last", [own, beside, passed, sums, scale]
    )
    cols_one = jnp.sum(cols[:, 1], axis=0)
    next_log_scale = math.log(target) - jnp.log(cols_one)
    return rebuilt, next_log_scale


def solution(mesh):
    sizes = (RING, RING, RING, RING, 2)
    rings = jax.sharding.Mesh(mesh.devices.reshape(sizes), ("x", "z_hi", "y", "z_lo", "core"))
    block, book = P(ITEMS, None), P(CODES, ITEMS)
    return jax.shard_map(
        shards,
        mesh=rings,
        in_specs=(block, block, book, book),
        out_specs=(P(ITEMS, CODES), P(CODES)),
        check_vma=False,
    )
```

```python
import functools
import math

import jax
import jax.numpy as jnp
from jax import lax
from jax.experimental import pallas as pl
from jax.experimental.pallas import tpu as pltpu
from jax.sharding import PartitionSpec as P

SWEEPS = 3
RING = 4
PLANE = ("x", "y")
CODES = ("z_lo", "core")
ITEMS = ("x", "z_hi", "y")
MIB = 1 << 20
STEP = 256
MOST = 48 * MIB
HBM = pl.BlockSpec(memory_space=pltpu.HBM)
FULL = pl.BlockSpec(memory_space=pltpu.VMEM)
BF16 = jnp.bfloat16
F32 = jnp.float32


def call(body, outs, name, ins, flops=0, nbytes=4 * MIB, limit=16 * MIB, scratch=(), out_specs=None):
    ins = [i if isinstance(i, tuple) else (i, FULL) for i in ins]
    specs = {} if out_specs is None else {"out_specs": out_specs}
    return pl.pallas_call(
        body,
        out_shape=outs,
        in_specs=[spec for _, spec in ins],
        scratch_shapes=list(scratch),
        compiler_params=pltpu.CompilerParams(vmem_limit_bytes=limit),
        cost_estimate=pl.CostEstimate(flops=flops, bytes_accessed=nbytes, transcendentals=0),
        name=name,
        **specs,
    )(*[array for array, _ in ins])


def shape(*sizes, of=F32):
    return jax.ShapeDtypeStruct(sizes, of)


def spread(rows, count):
    return jnp.broadcast_to(rows[None], (count,) + rows.shape)


def nt(a, b):
    return lax.dot_general(a, b, (((1,), (1,)), ((), ())), preferred_element_type=F32)


def nn(a, b):
    return jnp.dot(a, b, preferred_element_type=F32)


def k_rows(block, book, norms, inv_root):
    scores = nn(block, book)
    return jnp.exp((scores - norms) * inv_root).astype(BF16)


def fan_body(copies, column, two, one):
    run = column.shape[1] // 2
    for z in range(column.shape[0]):
        one[z] = column[z, run:, :]
        for i in range(copies):
            two[i, z] = column[z, :run, :]


def fetch_book(came, book, sems):
    fetches = []
    for x in range(RING):
        for y in range(RING):
            move = pltpu.make_async_copy(came.at[x * RING + y], book.at[x, :, y], sems.at[x * RING + y])
            move.start()
            fetches.append(move)
    return fetches


def half_norms(book, fetches):
    acc = jnp.zeros(book.shape[3:], F32)
    for x in range(RING):
        for y in range(RING):
            fetches[x * RING + y].wait()
            for z in range(RING):
                wide = book[x, z, y].astype(F32)
                acc = acc + wide * wide
    return 0.5 * jnp.sum(acc, axis=0, keepdims=True)


def make_k(inv_root, groups, start, came, block, k, total, book, held, sems, after_step=None):
    rows, features = held.shape
    codes = book.shape[-1]
    fetches = fetch_book(came, book, sems)
    loads = []
    for i in range(rows // STEP):
        here = pl.ds(i * STEP, STEP)
        there = pl.ds(start + i * STEP, STEP)
        loads.append(pltpu.make_async_copy(block.at[there], held.at[here], sems.at[len(fetches) + i]))
        loads[-1].start()
    norms = half_norms(book, fetches)
    ones = jnp.ones((16, codes), BF16)
    for i, load in enumerate(loads):
        here = slice(i * STEP, (i + 1) * STEP)
        load.wait()
        values = k_rows(held[here, :], book[...].reshape(features, codes), norms, inv_root)
        k[here, :] = values
        total[:, :, here] = spread(nt(ones, values)[0:1], groups)
        if after_step is not None:
            after_step(i)


def kernel_two_body(inv_root, groups, came, block, k_out, total, book, held, sems):
    make_k(inv_root, groups, 0, came, block, k_out, total, book, held, sems)


def kernel_one_body(inv_root, groups, start, came, block, after, k_out, total, book, held, k, sems, saved):
    saves = []

    def save(i):
        here = pl.ds(i * STEP, STEP)
        saves.append(pltpu.make_async_copy(k.at[here], k_out.at[here], saved.at[i]))
        saves[-1].start()

    make_k(inv_root, groups, start, came, block, k, total, book, held, sems, save)
    for move in saves:
        move.wait()


def two_terms(row):
    high = row.astype(BF16).astype(F32)
    at = lax.broadcasted_iota(jnp.int32, (16, row.shape[1]), 0)
    return jnp.where(at == 0, high, jnp.where(at == 1, row - high, 0.0)).astype(BF16)


def over_codes(scale, k):
    return jnp.sum(nt(two_terms(scale), k[...]), axis=0, keepdims=True)


def over_items(scale, k):
    return jnp.sum(nn(two_terms(scale), k[...]), axis=0, keepdims=True)


def col_body(copies, gathered, k, col_out, scale_out):
    scale = 1.0 / jnp.sum(gathered[...], axis=0)
    scale_out[...] = scale
    col_out[...] = spread(over_items(scale, k), copies)


def both_cols_body(copies, gathered, k, first, second, col_out, scale_out, held, sems):
    half = first.shape[0]
    fetches = []
    for i, part in enumerate((first, second)):
        fetches.append(pltpu.make_async_copy(part, held.at[pl.ds(i * half, half)], sems.at[i]))
        fetches[-1].start()
    scale = 1.0 / jnp.sum(gathered[...], axis=0)
    scale_out[...] = scale[0:1]
    col_out[:, 0:1, :] = spread(over_items(scale[0:1], k), copies)
    for fetch in fetches:
        fetch.wait()
    col_out[:, 1:2, :] = spread(over_items(scale[1:2], held), copies)


def row_body(target, groups, cols, k, *refs):
    out = refs[-1]
    scale = target / jnp.sum(cols[...], axis=0)[0:1]
    out[:, 0:1, :] = spread(over_codes(scale, k), groups)
    at = 0
    for more in refs[:-1]:
        out[:, 1:2, at : at + more.shape[2]] = more[...]
        at += more.shape[2]


def halves(row):
    high = row.astype(BF16)
    return high, (row - high.astype(F32)).astype(BF16)


def cut(row, width):
    return jnp.concatenate([row[:, i : i + width] for i in range(0, row.shape[1], width)], 0)


def pick(came, picked, parity):
    for x in range(RING):
        for y in range(RING):
            for z in range(2):
                picked[x, z, y] = came[x * RING + y, 2 * parity + z]


def transport_body(target, cols, r, k, came, t_out, other_out, sums_out, picked):
    rows, codes = k.shape
    wide = other_out.shape[1]
    scale = target / jnp.sum(cols[...], axis=0)[0:1]
    sums = over_codes(scale, k)
    sums_out[...] = sums
    pick(came, picked, 1 - lax.axis_index("core"))
    parts = jnp.concatenate([cut(part.astype(F32), wide) for part in halves(sums)], 0)
    filled = jnp.concatenate([parts, jnp.zeros((16 - parts.shape[0], wide), F32)], 0)
    other_out[rows : rows + 16, :] = filled.astype(BF16)
    r_up = jnp.transpose(jnp.broadcast_to(r[0:1, :], (8, r.shape[1])))
    for i in range(rows // STEP):
        here = slice(i * STEP, (i + 1) * STEP)
        t = (r_up[here, 0:1] * k[here, :].astype(F32) * scale).astype(BF16)
        t_out[here, :] = t
        other_out[here, :] = nt(t, picked[...].reshape(wide, codes)).astype(BF16)


def mine_body(t, came, out, picked):
    wide = out.shape[1]
    pick(came, picked, lax.axis_index("core"))
    for i in range(t.shape[0] // STEP):
        here = slice(i * STEP, (i + 1) * STEP)
        out[here, :] = nt(t[here, :], picked[...].reshape(wide, t.shape[1]))


def pack(sums):
    return jnp.concatenate([part.astype(F32) for part in halves(sums)], 0).astype(BF16)


def unpack(tail):
    tail = tail.astype(F32)
    return tail[:8] + tail[8:]


def pair_body(mine, came, sums, here_out, far_out, sums_out, cross_out, beside_out):
    rows, wide = mine.shape
    width = wide // RING
    tail = came[rows : rows + 16, :].astype(F32)
    n = rows // wide
    theirs = [tail[i : i + 1, :] + tail[n + i : n + i + 1, :] for i in range(n)]
    both = cut(sums[...] + jnp.concatenate(theirs, 1), width)
    sums_out[...] = both
    z = lax.axis_index("z_lo")
    pair = z + 1 - 2 * (z % 2)
    far = (z + 2) % RING
    for chip, out in ((z, here_out), (far, far_out), ((pair + 2) % RING, cross_out), (pair, beside_out)):
        lanes = pl.ds(pl.multiple_of(chip * width, width), width)
        value = mine[:, lanes] + came[:rows, lanes].astype(F32)
        out[:rows, :] = value.astype(out.dtype)
    cross_out[rows : rows + 16, :] = pack(both)


def cross_body(far, came, sums, out, sums_out):
    rows = far.shape[0]
    out[:rows, :] = (far[...] + came[:rows, :].astype(F32)).astype(BF16)
    both = sums[...] + unpack(came[rows : rows + 16, :])
    sums_out[...] = both
    out[rows : rows + 16, :] = pack(both)


def last_body(own, beside, far, sums, r, out):
    rows, width = out.shape
    total = sums[...] + unpack(far[rows : rows + 16, :])
    ratio = jnp.transpose(1.0 / (cut(r[0:1, :], width) * total))
    for i in range(rows // width):
        here = slice(i * width, (i + 1) * width)
        value = own[here, :] + beside[here, :].astype(F32) + far[here, :].astype(F32)
        out[here, :] = (value * ratio[:, i : i + 1]).astype(out.dtype)


def shards(block_two, block_one, codebook_two, codebook_one):
    rows, features = block_two.shape
    codes, run = codebook_two.shape
    groups = lax.axis_size(CODES)
    target = float(rows * lax.axis_size(ITEMS)) / float(codes * groups)
    inv_root = 1.0 / math.sqrt(features)
    book_flops = 2 * rows * features * codes

    plane = RING * RING
    sem = pltpu.SemaphoreType.DMA
    steps = rows // STEP
    both_books = spread(jnp.concatenate([codebook_two.T, codebook_one.T], 0), RING)
    column = lax.all_to_all(both_books, "z_hi", 0, 0)
    two, one = call(
        functools.partial(fan_body, plane),
        (shape(plane, RING, run, codes, of=BF16), shape(RING, run, codes, of=BF16)),
        "fan",
        [column],
    )
    came_two = lax.all_to_all(two, PLANE, 0, 0)
    came_two, one = lax.optimization_barrier((came_two, one))
    came_one = lax.all_gather(one, PLANE, axis=0, tiled=False)
    book_room = [
        pltpu.VMEM((RING, RING, RING, run, codes), BF16),
        pltpu.VMEM((rows, features), BF16),
    ]
    k_two, row_sums = call(
        functools.partial(kernel_two_body, inv_root, groups),
        (shape(rows, codes, of=BF16), shape(groups, 1, rows)),
        "kernel_two",
        [(came_two, HBM), (block_two, HBM)],
        flops=book_flops,
        limit=MOST + 4 * MIB - MIB // 4,
        scratch=book_room + [sem((plane + steps,))],
    )

    half = rows // 2

    def make_k_one(start, after):
        return call(
            functools.partial(kernel_one_body, inv_root, groups, start),
            (shape(half, codes, of=BF16), shape(groups, 1, half)),
            "kernel_one",
            [(came_one, HBM), (block_one, HBM), (after, HBM)],
            flops=book_flops // 2,
            limit=MOST + 4 * MIB,
            scratch=[
                book_room[0],
                pltpu.VMEM((half, features), BF16),
                pltpu.VMEM((half, codes), BF16),
                sem((plane + steps // 2,)),
                sem((steps // 2,)),
            ],
            out_specs=(HBM, FULL),
        )

    more = []
    small = 32 * rows * codes
    for sweep in range(SWEEPS):
        last = sweep == SWEEPS - 1
        n = 2 if last else 1
        gathered = lax.all_to_all(row_sums, CODES, 0, 0)
        outs = (shape(plane, n, codes), shape(1, rows))
        if last:
            col, scale = call(
                functools.partial(both_cols_body, plane),
                outs,
                "columns",
                [gathered, k_two] + [(part, HBM) for part in k_one],
                flops=small,
                limit=24 * MIB,
                scratch=[pltpu.VMEM((rows, codes), BF16), sem((2,))],
            )
        else:
            col, scale = call(
                functools.partial(col_body, plane), outs, "columns", [gathered, k_two], flops=small
            )
        col_all = lax.all_to_all(col, PLANE, 0, 0)
        if sweep == 1:
            first_k, first_one = make_k_one(0, col)
            col_all, first_one = lax.optimization_barrier((col_all, first_one))
        col = spread(jnp.sum(col_all, axis=0), RING)
        cols = lax.all_to_all(col, "z_hi", 0, 0)
        if sweep == 1:
            second_k, second_one = make_k_one(half, col)
            k_one, more = [first_k, second_k], [first_one, second_one]
        if not last:
            row_sums = call(
                functools.partial(row_body, target, groups),
                shape(groups, 2 if more else 1, rows),
                "rows",
                [cols, k_two] + more,
                flops=small,
            )

    wide = features // 2
    width = features // groups
    t, other, sums = call(
        functools.partial(transport_body, target),
        (shape(rows, codes, of=BF16), shape(rows + 16, wide, of=BF16), shape(1, rows)),
        "transport",
        [cols, scale, k_two, came_two],
        flops=book_flops // 2,
        limit=24 * MIB,
        scratch=[pltpu.VMEM((RING, 2, RING, run, codes), BF16)],
    )
    came = lax.ppermute(other, "core", [(0, 1), (1, 0)])
    mine = call(
        mine_body,
        shape(rows, wide),
        "mine",
        [t, came_two],
        flops=book_flops // 2,
        limit=24 * MIB,
        scratch=[pltpu.VMEM((RING, 2, RING, run, codes), BF16)],
    )
    tall = shape(rows + 16, width, of=BF16)
    own, far, sums, cross, beside = call(
        pair_body,
        (shape(rows, width), shape(rows, width), shape(8, width), tall, shape(rows, width, of=BF16)),
        "pair",
        [mine, came, sums],
        limit=24 * MIB,
    )
    neighbours = [(0, 1), (1, 0), (2, 3), (3, 2)]
    crossed = lax.ppermute(cross, "z_lo", neighbours)
    beside = lax.ppermute(beside, "z_lo", neighbours)
    passed, sums = call(cross_body, (tall, shape(8, width)), "cross", [far, crossed, sums])
    passed = lax.ppermute(passed, "z_lo", [(0, 2), (2, 0), (1, 3), (3, 1)])
    rebuilt = call(
        last_body, shape(rows, width, of=BF16), "last", [own, beside, passed, sums, scale]
    )
    cols_one = jnp.sum(cols[:, 1], axis=0)
    next_log_scale = math.log(target) - jnp.log(cols_one)
    return rebuilt, next_log_scale


def solution(mesh):
    sizes = (RING, RING, RING, RING, 2)
    rings = jax.sharding.Mesh(mesh.devices.reshape(sizes), ("x", "z_hi", "y", "z_lo", "core"))
    block, book = P(ITEMS, None), P(CODES, ITEMS)
    return jax.shard_map(
        shards,
        mesh=rings,
        in_specs=(block, block, book, book),
        out_specs=(P(ITEMS, CODES), P(CODES)),
        check_vma=False,
    )
```
